32 devices in a mesh: groups: 2 (over y), blk: 4 (over z), fsdp: 4 (over x, core).
Axes of the slice: x: 2, y: 2, z: 4, core: 2. Of those that a mesh axis runs over, the one named last changes fastest.
Arguments:
- hidden: bfloat16 [8192, 4096], P(('groups', 'blk', 'fsdp')), parts along dimension 0, may hold values from -6 to 6
- query: bfloat16 [8192, 4096], P(('groups', 'blk', 'fsdp')), parts along dimension 0, may hold values from -1024 to 1024
- out_grad: bfloat16 [8192, 4096], P(('groups', 'blk', 'fsdp')), parts along dimension 0, may hold values from -6 to 6
- lengths: int32 [128], P(('groups', 'blk', 'fsdp')), parts along dimension 0, may hold values from 16 to 63
- gain: float32 [4096], replicated, may hold values from 0.5 to 1.5
- w_key: bfloat16 [4096, 1024], P('fsdp'), may hold values from -0.09375 to 0.09375
- w_value: bfloat16 [4096, 1024], P('fsdp'), may hold values from -0.09375 to 0.09375
- proj_in: bfloat16 [4096, 32], replicated, may hold values from -0.09375 to 0.09375
- proj_out: bfloat16 [1024, 32], replicated, may hold values from -0.1875 to 0.1875
- test_feats: bfloat16 [512, 1024], P('blk'), may hold values from -0.75 to 0.75
Outputs:
- scores: float32 [128, 512], P(('groups', 'blk', 'fsdp')), parts along dimension 0
The draws below stay inside these ranges and needn't reach their ends.
There are 2 independent parts, one for each index of `groups`. The reference program is written for one: setup_inputs(seed, part) draws one part's arguments, and reference() takes and returns one part's arrays. A program takes and returns all parts, laid end to end along the dimension named above; an argument that names none is the same for every part. Nothing has to cross between parts.
All inputs are finite; a program needn't handle non-finite values.
Results may differ from the reference program's by a relative error of at most 0.011.
Values may be sent and summed in bfloat16 or wider, within the bound.
A program may use at most 128 MiB of HBM per device.

```python
import math
import jax
import jax.numpy as jnp
from jax import lax

D = 4096
HEADS = 32
KV_HEADS = 8
HEAD = 128
PROJ = 32
SEQ = 64
QW = 4096
KVW = 1024
FEAT = 1024
TOKENS = 4096
QUERIES = 512


def shared_lengths(key):
    length_key = jax.random.fold_in(key, 11)
    examples_here = TOKENS // SEQ
    drawn = jax.random.randint(length_key, (examples_here,), SEQ // 4, SEQ)
    drawn = drawn.at[0].set(SEQ - 1)
    drawn = drawn.at[1].set(SEQ // 4)
    return drawn.astype(jnp.int32)


def draw_lengths(key, part):
    return shared_lengths(key)


def draw_query(key, part):
    key = jax.random.fold_in(key, 3)
    noise_key = jax.random.fold_in(key, 0)
    drawn_draw = jax.random.truncated_normal(noise_key, -6.0, 6.0, (TOKENS, QW), jnp.float32)
    return drawn_draw.astype(jnp.bfloat16)


def draw_out_grad(key, part):
    key = jax.random.fold_in(key, 5)
    noise_key, scale_key = jax.random.split(key, 2)
    examples_here = TOKENS // SEQ
    exponents = jax.random.uniform(scale_key, (examples_here,), jnp.float32, -3.5, 0.5)
    example_scale = jnp.exp(exponents)
    drawn_draw = jax.random.truncated_normal(noise_key, -6.0, 6.0, (TOKENS, QW), jnp.float32)
    scaled = drawn_draw.reshape(examples_here, SEQ, QW) * example_scale[:, None, None]
    scaled = jnp.clip(scaled, -6.0, 6.0)
    return scaled.reshape(TOKENS, QW).astype(jnp.bfloat16)


def block_scale(key, shape, pieces, low, high):
    factor_of, own = 1.0, jax.random.fold_in(key, 6)
    for position, shards_of in pieces:
        heights = jnp.exp(jax.random.uniform(jax.random.fold_in(own, position), (shards_of,), jnp.float32, low / len(pieces), high / len(pieces)))
        factor_of = factor_of * jnp.repeat(heights, shape[position] // shards_of).reshape([-1 if axis == position else 1 for axis in range(len(shape))])
    return factor_of


def gaussian(key, shape, deviation, limit, cuts=(), kind=jnp.bfloat16):
    values = deviation * jax.random.normal(key, shape, jnp.float32)
    if cuts:
        values = values * block_scale(key, shape, cuts, -0.22, 0.18)
    return jnp.clip(values, -limit, limit).astype(kind)


def setup_inputs(seed: int = 0, part: int = 0) -> dict:
    key_list = jax.random.split(jax.random.key(seed), 11)
    part_keys = jax.random.split(jax.random.fold_in(key_list[10], part), 11)
    return {
        "hidden": gaussian(part_keys[0], (TOKENS, D), 1.0, 6.0, ((0, 16),)),
        "query": draw_query(jax.random.fold_in(jax.random.fold_in(key_list[10], part), 71), part),
        "out_grad": draw_out_grad(jax.random.fold_in(jax.random.fold_in(key_list[10], part), 71), part),
        "lengths": draw_lengths(jax.random.fold_in(jax.random.fold_in(key_list[10], part), 71), part),
        "gain": jnp.clip(1.0 + 0.1 * jax.random.normal(key_list[4], (D,), jnp.float32), 0.5, 1.5),
        "w_key": gaussian(key_list[5], (D, KVW), D ** -0.5, 0.09375, ((0, 4),)),
        "w_value": gaussian(key_list[6], (D, KVW), D ** -0.5, 0.09375, ((0, 4),)),
        "proj_in": gaussian(key_list[7], (D, PROJ), D ** -0.5, 0.09375),
        "proj_out": gaussian(key_list[8], (KVW, PROJ), KVW ** -0.5, 0.1875),
        "test_feats": gaussian(key_list[9], (QUERIES, FEAT), 0.05, 0.75, ((0, 4),)),
    }


norm_eps = 1e-05
rope_base = 500000.0
damping = 0.01

def swap_halves(block):
    middle = block.shape[-1] // 2
    return jnp.concatenate([block[..., middle:], block[..., :middle]], axis=-1)

def rope_tables():
    places = jnp.arange(SEQ).astype(jnp.float32)
    freqs = rope_base ** (-2.0 * jnp.arange(HEAD // 2).astype(jnp.float32) / HEAD)
    angles = places[:, None] * freqs[None, :]
    cosine = jnp.cos(angles)
    sine_tab = jnp.sin(angles)
    return (jnp.concatenate([cosine, cosine], -1), jnp.concatenate([-sine_tab, sine_tab], -1))

def normalize(hidden, gain):
    widened = hidden.astype(jnp.float32)
    inverse = lax.rsqrt(lax.optimization_barrier(jnp.mean(widened * widened, axis=1, keepdims=True)) + norm_eps)
    return (widened * inverse * gain).astype(jnp.bfloat16)

def features_of(normed, keys_raw, values_raw, query, out_grad, lengths, proj_in, proj_out):
    count = lengths.shape[0]
    group_size = HEADS // KV_HEADS
    cosine, sine_tab = rope_tables()
    keys_raw = keys_raw.reshape(count, SEQ, KV_HEADS, HEAD)
    keys_rot = (keys_raw * cosine[None, :, None, :] + swap_halves(keys_raw) * sine_tab[None, :, None, :]).astype(jnp.bfloat16)
    values = values_raw.reshape(count, SEQ, KV_HEADS, HEAD).astype(jnp.bfloat16)
    queries = query.reshape(count, SEQ, KV_HEADS, group_size, HEAD)
    places = jnp.arange(SEQ).astype(jnp.int32)
    inside = places[None, :] < lengths[:, None]
    grad_out = jnp.where(inside[:, :, None, None, None], out_grad.reshape(count, SEQ, KV_HEADS, group_size, HEAD), jnp.zeros((), jnp.bfloat16))
    inverse = 1.0 / math.sqrt(HEAD)
    logits = jnp.einsum('eskgh,etkh->ekgst', queries.astype(jnp.float32), keys_rot.astype(jnp.float32)) * inverse
    allowed = (places[:, None] >= places[None, :])[None, :, :] & inside[:, None, :]
    logits = jnp.where(allowed[:, None, None, :, :], logits, -1e+30)
    peak = lax.optimization_barrier(jnp.max(logits, axis=-1, keepdims=True))
    raised = jnp.exp(logits - peak)
    attn_prob = raised / lax.optimization_barrier(jnp.sum(raised, axis=-1, keepdims=True))
    grad_prob = jnp.einsum('eskgh,etkh->ekgst', grad_out.astype(jnp.float32), values.astype(jnp.float32))
    row_total = lax.optimization_barrier(jnp.sum(attn_prob * grad_prob, axis=-1, keepdims=True))
    grad_logit = (attn_prob * (grad_prob - row_total)).astype(jnp.bfloat16)
    grad_key = jnp.einsum('ekgst,eskgh->etkh', grad_logit.astype(jnp.float32), queries.astype(jnp.float32)) * inverse
    grad_key = grad_key * cosine[None, :, None, :] + swap_halves(grad_key * sine_tab[None, :, None, :])
    grad_key = grad_key.astype(jnp.bfloat16).reshape(count * SEQ, KV_HEADS * HEAD)
    left_fac = jnp.dot(grad_key.astype(jnp.float32), proj_out.astype(jnp.float32), preferred_element_type=jnp.float32).reshape(count, SEQ, PROJ)
    right_fac = jnp.dot(normed.astype(jnp.float32), proj_in.astype(jnp.float32), preferred_element_type=jnp.float32).reshape(count, SEQ, PROJ)
    features = jnp.einsum('eti,etj->eij', left_fac, right_fac, precision=lax.Precision.HIGHEST)
    return features.reshape(count, PROJ * PROJ)

def precondition(gram, features):
    mean_diag = jnp.trace(gram) / (PROJ * PROJ) + 1e-06
    system = gram / mean_diag + damping * jnp.eye(PROJ * PROJ, dtype=jnp.float32)
    factor = jnp.linalg.cholesky(system)
    return jax.scipy.linalg.cho_solve((factor, True), features.T).T

def reference(hidden, query, out_grad, lengths, gain, w_key, w_value, proj_in, proj_out, test_feats):
    normed = normalize(hidden, gain)
    keys_raw = jnp.dot(normed.astype(jnp.float32), w_key.astype(jnp.float32), preferred_element_type=jnp.float32)
    values_raw = jnp.dot(normed.astype(jnp.float32), w_value.astype(jnp.float32), preferred_element_type=jnp.float32)
    features = features_of(normed, keys_raw, values_raw, query, out_grad, lengths, proj_in, proj_out)
    gram = jnp.dot(features.T.astype(jnp.float32), features.astype(jnp.float32), precision=lax.Precision.HIGHEST, preferred_element_type=jnp.float32)
    weighted = precondition(gram, features)
    return jnp.dot(weighted.astype(jnp.float32), test_feats.astype(jnp.float32).T.astype(jnp.float32), precision=lax.Precision.HIGHEST, preferred_element_type=jnp.float32)
```

```python
import math

import jax
import jax.numpy as jnp
from jax import lax
from jax.experimental import pallas as pl
from jax.experimental.pallas import tpu as pltpu
from jax.sharding import PartitionSpec as P

HEADS = 32
KV_HEADS = 8
HEAD = 128
PROJ = 32
SEQ = 64


norm_eps = 1e-05
rope_base = 500000.0
damping = 0.01


def swap_halves(block):
    middle = block.shape[-1] // 2
    return jnp.concatenate([block[..., middle:], block[..., :middle]], axis=-1)


def rope_tables():
    places = jnp.arange(SEQ).astype(jnp.float32)
    freqs = rope_base ** (-2.0 * jnp.arange(HEAD // 2).astype(jnp.float32) / HEAD)
    angles = places[:, None] * freqs[None, :]
    cosine = jnp.cos(angles)
    sine_tab = jnp.sin(angles)
    return (jnp.concatenate([cosine, cosine], -1), jnp.concatenate([-sine_tab, sine_tab], -1))


def normalize(hidden, gain):
    widened = hidden.astype(jnp.float32)
    inverse = lax.rsqrt(jnp.mean(widened * widened, axis=1, keepdims=True) + norm_eps)
    return (widened * inverse * gain).astype(jnp.bfloat16)


def features_of(normed, keys_raw, values_raw, query, out_grad, lengths, proj_in, proj_out):
    count = lengths.shape[0]
    group_size = HEADS // KV_HEADS
    cosine, sine_tab = rope_tables()
    keys_raw = keys_raw.reshape(count, SEQ, KV_HEADS, HEAD)
    keys_rot = (
        keys_raw * cosine[None, :, None, :] + swap_halves(keys_raw) * sine_tab[None, :, None, :]
    ).astype(jnp.bfloat16)
    values = values_raw.reshape(count, SEQ, KV_HEADS, HEAD).astype(jnp.bfloat16)
    queries = query.reshape(count, SEQ, KV_HEADS, group_size, HEAD)
    places = jnp.arange(SEQ)
    inside = places[None, :] < lengths[:, None]
    grad_out = jnp.where(
        inside[:, :, None, None, None],
        out_grad.reshape(count, SEQ, KV_HEADS, group_size, HEAD),
        jnp.zeros((), jnp.bfloat16),
    )
    inverse = 1.0 / math.sqrt(HEAD)
    logits = (
        jnp.einsum("eskgh,etkh->ekgst", queries, keys_rot, preferred_element_type=jnp.float32)
        * inverse
    )
    allowed = (places[:, None] >= places[None, :])[None, :, :] & inside[:, None, :]
    logits = jnp.where(allowed[:, None, None, :, :], logits, -1e30)
    peak = jnp.max(logits, axis=-1, keepdims=True)
    raised = jnp.exp(logits - peak)
    attn_prob = raised / jnp.sum(raised, axis=-1, keepdims=True)
    grad_prob = jnp.einsum(
        "eskgh,etkh->ekgst", grad_out, values, preferred_element_type=jnp.float32
    )
    row_total = jnp.sum(attn_prob * grad_prob, axis=-1, keepdims=True)
    grad_logit = (attn_prob * (grad_prob - row_total)).astype(jnp.bfloat16)
    grad_key = (
        jnp.einsum("ekgst,eskgh->etkh", grad_logit, queries, preferred_element_type=jnp.float32)
        * inverse
    )
    grad_key = grad_key * cosine[None, :, None, :] + swap_halves(
        grad_key * sine_tab[None, :, None, :]
    )
    grad_key = grad_key.astype(jnp.bfloat16).reshape(count * SEQ, KV_HEADS * HEAD)
    left_fac = jnp.dot(grad_key, proj_out, preferred_element_type=jnp.float32).reshape(
        count, SEQ, PROJ
    )
    right_fac = jnp.dot(normed, proj_in, preferred_element_type=jnp.float32).reshape(
        count, SEQ, PROJ
    )
    features = jnp.einsum("eti,etj->eij", left_fac, right_fac, precision=lax.Precision.HIGHEST)
    return features.reshape(count, PROJ * PROJ)


HIGHEST = lax.Precision.HIGHEST
CONTRACT_LAST = (((1,), (1,)), ((), ()))


def sweep(system, row, col, k, lanes, subs):
    pivot = 1.0 / jnp.sum(jnp.where(lanes[:1] == k, row, 0.0), axis=1, keepdims=True)
    row = jnp.where(lanes[:1] == k, pivot, row * pivot)
    col = jnp.where(subs[:, :1] == k, -1.0, col)
    return jnp.where((lanes == k) | (subs == k), 0.0, system) - col * row


def score_kernel(feat_ref, test_ref, out_ref, inv_ref):
    count = feat_ref.shape[0]
    width = feat_ref.shape[1]
    mine = out_ref.shape[0]
    first = (lax.axis_index("blk") * lax.axis_size("fsdp") + lax.axis_index("fsdp")) * mine
    feats = feat_ref[...]
    gram = lax.dot_general(
        feats, feats, CONTRACT_LAST, precision=HIGHEST, preferred_element_type=jnp.float32
    )
    lanes = lax.broadcasted_iota(jnp.int32, (count, count), 1)
    subs = lax.broadcasted_iota(jnp.int32, (count, count), 0)
    diagonal = lanes == subs
    mean_diag = jnp.sum(jnp.where(diagonal, gram, 0.0), keepdims=True) / width + 1e-06
    system = gram / mean_diag + jnp.where(diagonal, damping, 0.0)
    if count <= 128:
        for k in range(count):
            system = sweep(system, system[k : k + 1, :], system[:, k : k + 1], k, lanes, subs)
        inv_ref[...] = system
    else:
        inv_ref[...] = system

        def step(k, carry):
            now = inv_ref[...]
            col = jnp.sum(jnp.where(lanes == k, now, 0.0), axis=1, keepdims=True)
            inv_ref[...] = sweep(now, inv_ref[pl.ds(k, 1), :], col, k, lanes, subs)
            return carry

        lax.fori_loop(0, count, step, 0)
    chosen = lax.broadcasted_iota(jnp.int32, (mine, count), 1) == (
        lax.broadcasted_iota(jnp.int32, (mine, count), 0) + first
    )
    rows = lax.dot_general(
        chosen.astype(jnp.float32),
        inv_ref[...],
        (((1,), (0,)), ((), ())),
        precision=HIGHEST,
        preferred_element_type=jnp.float32,
    )
    weighted = jnp.dot(rows, feats, precision=HIGHEST, preferred_element_type=jnp.float32)
    total = None
    for _ in range(3):
        piece = weighted.astype(jnp.bfloat16)
        weighted = weighted - piece.astype(jnp.float32)
        term = lax.dot_general(
            piece, test_ref[...], CONTRACT_LAST, preferred_element_type=jnp.float32
        )
        total = term if total is None else total + term
    out_ref[...] = total


def score(every_feat, tests, mine):
    count = every_feat.shape[0]
    return pl.pallas_call(
        score_kernel,
        out_shape=jax.ShapeDtypeStruct((mine, tests.shape[0]), jnp.float32),
        in_specs=[pl.BlockSpec(memory_space=pltpu.VMEM)] * 2,
        out_specs=pl.BlockSpec(memory_space=pltpu.VMEM),
        scratch_shapes=[pltpu.VMEM((count, count), jnp.float32)],
        compiler_params=pltpu.CompilerParams(vmem_limit_bytes=48 * 1024 * 1024),
    )(every_feat, tests)


def on_device(
    hidden, query, out_grad, lengths, gain, w_key, w_value, proj_in, proj_out, test_feats
):
    normed = normalize(hidden, gain)
    keys_raw = jnp.dot(
        normed,
        lax.all_gather(w_key, "fsdp", axis=0, tiled=True),
        preferred_element_type=jnp.float32,
    )
    values_raw = jnp.dot(
        normed,
        lax.all_gather(w_value, "fsdp", axis=0, tiled=True),
        preferred_element_type=jnp.float32,
    )
    features = features_of(
        normed, keys_raw, values_raw, query, out_grad, lengths, proj_in, proj_out
    )
    every_feat = lax.all_gather(features, ("blk", "fsdp"), axis=0, tiled=True)
    tests = lax.all_gather(test_feats, "blk", axis=0, tiled=True)
    return score(every_feat, tests, features.shape[0])


def solution(mesh):
    in_specs = (
        P(("groups", "blk", "fsdp"), None),
        P(("groups", "blk", "fsdp"), None),
        P(("groups", "blk", "fsdp"), None),
        P(("groups", "blk", "fsdp")),
        P(),
        P("fsdp", None),
        P("fsdp", None),
        P(),
        P(),
        P("blk", None),
    )
    out_specs = P(("groups", "blk", "fsdp"), None)
    return jax.shard_map(
        on_device, mesh=mesh, in_specs=in_specs, out_specs=out_specs, check_vma=False
    )
```

```python
import math

import jax
import jax.numpy as jnp
import numpy as np
from jax import lax
from jax.experimental import pallas as pl
from jax.experimental.pallas import tpu as pltpu
from jax.sharding import PartitionSpec as P

HEADS = 32
KV_HEADS = 8
HEAD = 128
PROJ = 32
SEQ = 64


norm_eps = 1e-05
rope_base = 500000.0
damping = 0.01
GROUP = HEADS // KV_HEADS
AHEAD = 2


def rope_tables(count):
    freqs = rope_base ** (-2.0 * np.arange(HEAD // 2) / HEAD)
    angles = np.arange(SEQ)[:, None] * freqs[None, :]
    cosine, sine = np.cos(angles), np.sin(angles)
    cosine = np.concatenate([cosine, cosine], -1)
    sine = np.concatenate([-sine, sine], -1)
    return [np.tile(table, (count, 1)).astype(np.float32) for table in (cosine, sine)]


HIGHEST = lax.Precision.HIGHEST
CONTRACT_LAST = (((1,), (1,)), ((), ()))


def sweep(system, row, col, k, lanes, subs):
    pivot = 1.0 / jnp.sum(jnp.where(lanes[:1] == k, row, 0.0), axis=1, keepdims=True)
    row = jnp.where(lanes[:1] == k, pivot, row * pivot)
    col = jnp.where(subs[:, :1] == k, -1.0, col)
    return jnp.where((lanes == k) | (subs == k), 0.0, system) - col * row


def score_kernel(feat_ref, test_ref, out_ref, inv_ref):
    count = feat_ref.shape[0]
    width = feat_ref.shape[1]
    mine = out_ref.shape[0]
    first = (lax.axis_index("blk") * lax.axis_size("fsdp") + lax.axis_index("fsdp")) * mine
    feats = feat_ref[...]
    gram = lax.dot_general(
        feats, feats, CONTRACT_LAST, precision=HIGHEST, preferred_element_type=jnp.float32
    )
    lanes = lax.broadcasted_iota(jnp.int32, (count, count), 1)
    subs = lax.broadcasted_iota(jnp.int32, (count, count), 0)
    diagonal = lanes == subs
    mean_diag = jnp.sum(jnp.where(diagonal, gram, 0.0), keepdims=True) / width + 1e-06
    system = gram / mean_diag + jnp.where(diagonal, damping, 0.0)
    if count <= 128:
        for k in range(count):
            system = sweep(system, system[k : k + 1, :], system[:, k : k + 1], k, lanes, subs)
        inv_ref[...] = system
    else:
        inv_ref[...] = system

        def step(k, carry):
            now = inv_ref[...]
            col = jnp.sum(jnp.where(lanes == k, now, 0.0), axis=1, keepdims=True)
            inv_ref[...] = sweep(now, inv_ref[pl.ds(k, 1), :], col, k, lanes, subs)
            return carry

        lax.fori_loop(0, count, step, 0)
    chosen = lax.broadcasted_iota(jnp.int32, (mine, count), 1) == (
        lax.broadcasted_iota(jnp.int32, (mine, count), 0) + first
    )
    rows = lax.dot_general(
        chosen.astype(jnp.float32),
        inv_ref[...],
        (((1,), (0,)), ((), ())),
        precision=HIGHEST,
        preferred_element_type=jnp.float32,
    )
    weighted = jnp.dot(rows, feats, precision=HIGHEST, preferred_element_type=jnp.float32)
    total = None
    for _ in range(3):
        piece = weighted.astype(jnp.bfloat16)
        weighted = weighted - piece.astype(jnp.float32)
        term = lax.dot_general(
            piece, test_ref[...], CONTRACT_LAST, preferred_element_type=jnp.float32
        )
        total = term if total is None else total + term
    out_ref[...] = total


def score(every_feat, tests, mine):
    count = every_feat.shape[0]
    return pl.pallas_call(
        score_kernel,
        out_shape=jax.ShapeDtypeStruct((mine, tests.shape[0]), jnp.float32),
        in_specs=[pl.BlockSpec(memory_space=pltpu.VMEM)] * 2,
        out_specs=pl.BlockSpec(memory_space=pltpu.VMEM),
        scratch_shapes=[pltpu.VMEM((count, count), jnp.float32)],
        compiler_params=pltpu.CompilerParams(vmem_limit_bytes=48 * 1024 * 1024),
    )(every_feat, tests)


def feature_kernel(
    hidden_ref, query_ref, outg_ref, keep_ref, gain_ref, wk_ref, wv_ref, pin_ref, pout_ref,
    cos_ref, sin_ref, out_ref,
    wbuf, hid, que, outg, normed, left, right,
    in_sem, own_sem, sib_send, sib_recv, x_send, x_recv, y_send, y_recv,
    fx_send, fx_recv, fy_send, fy_recv,
):
    count = out_ref.shape[0]
    rows = wk_ref.shape[0]
    half_rows = rows // 2
    inverse = 1.0 / math.sqrt(HEAD)
    g = lax.axis_index("groups")
    f = lax.axis_index("fsdp")
    sib = f + 1 - 2 * (f % 2)
    across = (f + 2) % 4
    beyond = (sib + 2) % 4
    other = g + 1 - 2 * (g % 2)
    half = g % 2

    def rows_of(owner, part):
        return pl.ds(pl.multiple_of(owner * rows + part * half_rows, half_rows), half_rows)

    def copy(h, where, send, recv, to):
        part = wbuf.at[h, :, where, :]
        return pltpu.make_async_remote_copy(
            src_ref=part, dst_ref=part, send_sem=send.at[h], recv_sem=recv.at[h],
            device_id=to, device_id_type=pl.DeviceIdType.MESH,
        )

    whole_own = pl.ds(pl.multiple_of(f * rows, rows), rows)
    whole_sib = pl.ds(pl.multiple_of(sib * rows, rows), rows)
    to_sib, to_across, to_other = {"fsdp": sib}, {"fsdp": across}, {"groups": other}

    def own(h, kind):
        return pltpu.make_async_copy(
            (wk_ref, wv_ref)[kind].at[:, pl.ds(pl.multiple_of(h * HEAD, HEAD), HEAD)],
            wbuf.at[h, kind, whole_own, :],
            own_sem.at[kind, h],
        )

    def send_own(h):
        own(h, 0).wait()
        own(h, 1).wait()
        copy(h, rows_of(f, half), x_send, x_recv, to_across).start()
        copy(h, whole_own, sib_send, sib_recv, to_sib).start()

    def start_own(h, carry):
        own(h, 0).start()
        own(h, 1).start()
        return carry

    lax.fori_loop(0, KV_HEADS, start_own, 0)
    loads = [
        pltpu.make_async_copy(src, dst, in_sem.at[i])
        for i, (src, dst) in enumerate(((hidden_ref, hid), (query_ref, que), (outg_ref, outg)))
    ]
    for load in loads:
        load.start()

    barrier = pltpu.get_barrier_semaphore()
    for to in (to_sib, to_across, to_other):
        pl.semaphore_signal(barrier, inc=1, device_id=to, device_id_type=pl.DeviceIdType.MESH)
    pl.semaphore_wait(barrier, 3)
    for h in range(AHEAD):
        send_own(h)

    loads[0].wait()
    strip = 16

    def normalize(i, carry):
        where = pl.ds(pl.multiple_of(i * strip, strip), strip)
        widened = hid[where, :].astype(jnp.float32)
        scale = lax.rsqrt(jnp.mean(widened * widened, axis=1, keepdims=True) + norm_eps)
        normed[where, :] = (widened * scale * gain_ref[...]).astype(jnp.bfloat16)
        return carry

    lax.fori_loop(0, hid.shape[0] // strip, normalize, 0)
    right[...] = jnp.dot(normed[...], pin_ref[...], preferred_element_type=jnp.float32)
    left[...] = jnp.zeros_like(left)
    loads[1].wait()
    loads[2].wait()

    def stack(ref, e, h):
        block = ref[e * SEQ : (e + 1) * SEQ, pl.ds(pl.multiple_of(h * GROUP * HEAD, HEAD), GROUP * HEAD)]
        return jnp.concatenate([block[:, i * HEAD : (i + 1) * HEAD] for i in range(GROUP)], axis=0)

    def head(h):
        weights = jnp.concatenate([wbuf[h, 0], wbuf[h, 1]], axis=1)
        both = jnp.dot(normed[...], weights, preferred_element_type=jnp.float32)
        cosine, sine = cos_ref[...], sin_ref[...]
        keys = both[:, :HEAD]
        keys = (keys * cosine + pltpu.roll(keys, HEAD // 2, 1) * sine).astype(jnp.bfloat16)
        values = both[:, HEAD:].astype(jnp.bfloat16)
        causal = lax.broadcasted_iota(jnp.int32, (SEQ, GROUP * SEQ), 0) <= (
            lax.broadcasted_iota(jnp.int32, (SEQ, GROUP * SEQ), 1) % SEQ
        )
        grads = []
        for e in range(count):
            mine = slice(e * SEQ, (e + 1) * SEQ)
            queries = stack(que, e, h)
            logits = lax.dot_general(
                keys[mine], queries, CONTRACT_LAST, preferred_element_type=jnp.float32
            ) * inverse
            logits = jnp.where(causal, logits, -1e30)
            raised = jnp.exp(logits - jnp.max(logits, axis=0, keepdims=True))
            prob = raised / jnp.sum(raised, axis=0, keepdims=True)
            grad_prob = lax.dot_general(
                values[mine], stack(outg, e, h), CONTRACT_LAST, preferred_element_type=jnp.float32
            ) * keep_ref[e : e + 1, :]
            total = jnp.sum(prob * grad_prob, axis=0, keepdims=True)
            grad_logit = (prob * (grad_prob - total)).astype(jnp.bfloat16)
            grads.append(jnp.dot(grad_logit, queries, preferred_element_type=jnp.float32))
        grad = jnp.concatenate(grads, axis=0) * inverse
        grad = grad * cosine + pltpu.roll(grad * sine, HEAD // 2, 1)
        block = pout_ref[pl.ds(pl.multiple_of(h * HEAD, HEAD), HEAD), :]
        left[...] += jnp.dot(grad.astype(jnp.bfloat16), block, preferred_element_type=jnp.float32)

    def step(i, carry):
        @pl.when(i < KV_HEADS)
        def _():
            copy(i, rows_of(across, half), x_send, x_recv, to_across).wait_recv()
            copy(i, rows_of(across, half), y_send, y_recv, to_other).start()
            copy(i, rows_of(across, half), fx_send, fx_recv, to_sib).start()

        @pl.when(i + AHEAD < KV_HEADS)
        def _():
            send_own(i + AHEAD)

        @pl.when((i >= 1) & (i <= KV_HEADS))
        def _():
            copy(i - 1, rows_of(across, 1 - half), y_send, y_recv, to_other).wait_recv()
            copy(i - 1, rows_of(across, 1 - half), fy_send, fy_recv, to_sib).start()

        @pl.when(i >= 2)
        def _():
            h = i - 2
            copy(h, whole_sib, sib_send, sib_recv, to_sib).wait_recv()
            copy(h, rows_of(beyond, half), fx_send, fx_recv, to_sib).wait_recv()
            copy(h, rows_of(beyond, 1 - half), fy_send, fy_recv, to_sib).wait_recv()
            head(h)

        return carry

    lax.fori_loop(0, KV_HEADS + 2, step, 0)

    def finish(h, carry):
        copy(h, rows_of(f, half), x_send, x_recv, to_across).wait_send()
        copy(h, whole_own, sib_send, sib_recv, to_sib).wait_send()
        copy(h, rows_of(across, half), y_send, y_recv, to_other).wait_send()
        copy(h, rows_of(across, half), fx_send, fx_recv, to_sib).wait_send()
        copy(h, rows_of(across, 1 - half), fy_send, fy_recv, to_sib).wait_send()
        return carry

    lax.fori_loop(0, KV_HEADS, finish, 0)
    shape = left.shape
    belongs = lax.broadcasted_iota(jnp.int32, shape, 0) // SEQ == (
        lax.broadcasted_iota(jnp.int32, shape, 1) % count
    )
    outer = lax.dot_general(
        jnp.where(belongs, left[...], 0.0),
        right[...],
        (((0,), (0,)), ((), ())),
        precision=HIGHEST,
        preferred_element_type=jnp.float32,
    )
    for i in range(PROJ):
        out_ref[:, i * PROJ : (i + 1) * PROJ] = outer[i * count : (i + 1) * count, :]


def features_of(hidden, query, out_grad, lengths, gain, w_key, w_value, proj_in, proj_out):
    count = lengths.shape[0]
    tokens, width = hidden.shape
    keep = (jnp.arange(SEQ)[None, :] < lengths[:, None]).astype(jnp.float32)
    cosine, sine = rope_tables(count)
    anywhere = pl.BlockSpec(memory_space=pl.ANY)
    vmem = pl.BlockSpec(memory_space=pltpu.VMEM)
    heads = pltpu.SemaphoreType.DMA((KV_HEADS,))
    return pl.pallas_call(
        feature_kernel,
        out_shape=jax.ShapeDtypeStruct((count, PROJ * PROJ), jnp.float32),
        in_specs=[anywhere] * 3 + [vmem] * 2 + [anywhere] * 2 + [vmem] * 4,
        out_specs=vmem,
        scratch_shapes=[
            pltpu.VMEM((KV_HEADS, 2, width, HEAD), jnp.bfloat16),
            pltpu.VMEM((tokens, width), jnp.bfloat16),
            pltpu.VMEM((tokens, query.shape[1]), jnp.bfloat16),
            pltpu.VMEM((tokens, query.shape[1]), jnp.bfloat16),
            pltpu.VMEM((tokens, width), jnp.bfloat16),
            pltpu.VMEM((tokens, PROJ * count), jnp.float32),
            pltpu.VMEM((tokens, PROJ), jnp.float32),
            pltpu.SemaphoreType.DMA((3,)),
            pltpu.SemaphoreType.DMA((2, KV_HEADS)),
        ]
        + [heads] * 10,
        compiler_params=pltpu.CompilerParams(
            collective_id=0, has_side_effects=True, vmem_limit_bytes=56 * 1024 * 1024
        ),
        cost_estimate=pl.CostEstimate(
            flops=2 * tokens * width * 2 * KV_HEADS * HEAD, bytes_accessed=100_000_000, transcendentals=0
        ),
    )(
        hidden, query, out_grad, jnp.tile(keep, (1, GROUP)), gain.reshape(1, width), w_key, w_value,
        proj_in, jnp.repeat(proj_out, count, axis=1), cosine, sine,
    )


def on_device(
    hidden, query, out_grad, lengths, gain, w_key, w_value, proj_in, proj_out, test_feats
):
    features = features_of(
        hidden, query, out_grad, lengths, gain, w_key, w_value, proj_in, proj_out
    )
    every_feat = lax.all_gather(features, ("blk", "fsdp"), axis=0, tiled=True)
    tests = lax.all_gather(test_feats, "blk", axis=0, tiled=True)
    return score(every_feat, tests, features.shape[0])


def solution(mesh):
    in_specs = (
        P(("groups", "blk", "fsdp"), None),
        P(("groups", "blk", "fsdp"), None),
        P(("groups", "blk", "fsdp"), None),
        P(("groups", "blk", "fsdp")),
        P(),
        P("fsdp", None),
        P("fsdp", None),
        P(),
        P(),
        P("blk", None),
    )
    out_specs = P(("groups", "blk", "fsdp"), None)
    return jax.shard_map(
        on_device, mesh=mesh, in_specs=in_specs, out_specs=out_specs, check_vma=False
    )
```

```python
import math

import jax
import jax.numpy as jnp
import numpy as np
from jax import lax
from jax.experimental import pallas as pl
from jax.experimental.pallas import tpu as pltpu
from jax.sharding import PartitionSpec as P

HEADS = 32
KV_HEADS = 8
HEAD = 128
PROJ = 32
SEQ = 64


norm_eps = 1e-05
rope_base = 500000.0
damping = 0.01
GROUP = HEADS // KV_HEADS
AHEAD = 2


def rope_tables(count):
    freqs = rope_base ** (-2.0 * np.arange(HEAD // 2) / HEAD)
    angles = np.arange(SEQ)[:, None] * freqs[None, :]
    cosine, sine = np.cos(angles), np.sin(angles)
    cosine = np.concatenate([cosine, cosine], -1)
    sine = np.concatenate([-sine, sine], -1)
    return [np.tile(table, (count, 1)).astype(np.float32) for table in (cosine, sine)]


HIGHEST = lax.Precision.HIGHEST
CONTRACT_LAST = (((1,), (1,)), ((), ()))


def sweep(system, row, col, k, lanes, subs):
    pivot = 1.0 / jnp.sum(jnp.where(lanes[:1] == k, row, 0.0), axis=1, keepdims=True)
    row = jnp.where(lanes[:1] == k, pivot, row * pivot)
    col = jnp.where(subs[:, :1] == k, -1.0, col)
    return jnp.where((lanes == k) | (subs == k), 0.0, system) - col * row


def score(feats, tests, inv_ref, first, mine):
    count, width = feats.shape
    gram = lax.dot_general(
        feats, feats, CONTRACT_LAST, precision=HIGHEST, preferred_element_type=jnp.float32
    )
    lanes = lax.broadcasted_iota(jnp.int32, (count, count), 1)
    subs = lax.broadcasted_iota(jnp.int32, (count, count), 0)
    diagonal = lanes == subs
    mean_diag = jnp.sum(jnp.where(diagonal, gram, 0.0), keepdims=True) / width + 1e-06
    system = gram / mean_diag + jnp.where(diagonal, damping, 0.0)
    if count <= 128:
        for k in range(count):
            system = sweep(system, system[k : k + 1, :], system[:, k : k + 1], k, lanes, subs)
        inv_ref[...] = system
    else:
        inv_ref[...] = system

        def step(k, carry):
            now = inv_ref[...]
            col = jnp.sum(jnp.where(lanes == k, now, 0.0), axis=1, keepdims=True)
            inv_ref[...] = sweep(now, inv_ref[pl.ds(k, 1), :], col, k, lanes, subs)
            return carry

        lax.fori_loop(0, count, step, 0)
    chosen = lax.broadcasted_iota(jnp.int32, (mine, count), 1) == (
        lax.broadcasted_iota(jnp.int32, (mine, count), 0) + first
    )
    rows = lax.dot_general(
        chosen.astype(jnp.float32),
        inv_ref[...],
        (((1,), (0,)), ((), ())),
        precision=HIGHEST,
        preferred_element_type=jnp.float32,
    )
    weighted = jnp.dot(rows, feats, precision=HIGHEST, preferred_element_type=jnp.float32)
    total = None
    for _ in range(3):
        piece = weighted.astype(jnp.bfloat16)
        weighted = weighted - piece.astype(jnp.float32)
        term = lax.dot_general(
            piece, tests, CONTRACT_LAST, preferred_element_type=jnp.float32
        )
        total = term if total is None else total + term
    return total


def score_kernel(
    hidden_ref, query_ref, outg_ref, len_ref, gain_ref, wk_ref, wv_ref, pin_ref, pout_ref,
    test_ref, cos_ref, sin_ref, out_ref,
    wbuf, hid, que, outg, normed, left, right, fbuf, flat, tests, inv_ref,
    in_sem, own_sem, sib_send, sib_recv, x_send, x_recv, y_send, y_recv,
    fx_send, fx_recv, fy_send, fy_recv,
    t_sem, t_send, t_recv, a_send, a_recv, b_send, b_recv,
):
    count = len_ref.shape[0]
    rows = wk_ref.shape[0]
    half_rows = rows // 2
    inverse = 1.0 / math.sqrt(HEAD)
    g = lax.axis_index("groups")
    f = lax.axis_index("fsdp")
    sib = f + 1 - 2 * (f % 2)
    across = (f + 2) % 4
    beyond = (sib + 2) % 4
    other = g + 1 - 2 * (g % 2)
    half = g % 2
    b = lax.axis_index("blk")
    blocks = lax.axis_size("blk")
    block_rows = test_ref.shape[0]
    MESH = pl.DeviceIdType.MESH

    def to_block(k):
        return {"blk": (b + k) % blocks}

    def test_copy(k):
        where = pl.ds(pl.multiple_of(b * block_rows, block_rows), block_rows)
        return pltpu.make_async_remote_copy(
            src_ref=test_ref, dst_ref=tests.at[where, :], send_sem=t_send.at[k],
            recv_sem=t_recv.at[k], device_id=to_block(k), device_id_type=MESH,
        )

    def feat_copy(k):
        part = fbuf.at[f * blocks + b]
        return pltpu.make_async_remote_copy(
            src_ref=part, dst_ref=part, send_sem=a_send.at[k],
            recv_sem=a_recv.at[k], device_id=to_block(k), device_id_type=MESH,
        )

    def spread_copy(k):
        part = fbuf.at[pl.ds(f * blocks, blocks)]
        return pltpu.make_async_remote_copy(
            src_ref=part, dst_ref=part, send_sem=b_send.at[k],
            recv_sem=b_recv.at[k], device_id={"fsdp": (f + k) % 4}, device_id_type=MESH,
        )

    def rows_of(owner, part):
        return pl.ds(pl.multiple_of(owner * rows + part * half_rows, half_rows), half_rows)

    def copy(h, where, send, recv, to):
        part = wbuf.at[h, :, where, :]
        return pltpu.make_async_remote_copy(
            src_ref=part, dst_ref=part, send_sem=send.at[h], recv_sem=recv.at[h],
            device_id=to, device_id_type=pl.DeviceIdType.MESH,
        )

    whole_own = pl.ds(pl.multiple_of(f * rows, rows), rows)
    whole_sib = pl.ds(pl.multiple_of(sib * rows, rows), rows)
    to_sib, to_across, to_other = {"fsdp": sib}, {"fsdp": across}, {"groups": other}

    def own(h, kind):
        return pltpu.make_async_copy(
            (wk_ref, wv_ref)[kind].at[:, pl.ds(pl.multiple_of(h * HEAD, HEAD), HEAD)],
            wbuf.at[h, kind, whole_own, :],
            own_sem.at[kind, h],
        )

    def send_own(h):
        own(h, 0).wait()
        own(h, 1).wait()
        copy(h, rows_of(f, half), x_send, x_recv, to_across).start()
        copy(h, whole_own, sib_send, sib_recv, to_sib).start()

    def start_own(h, carry):
        own(h, 0).start()
        own(h, 1).start()
        return carry

    lax.fori_loop(0, KV_HEADS, start_own, 0)
    loads = [
        pltpu.make_async_copy(src, dst, in_sem.at[i])
        for i, (src, dst) in enumerate(((hidden_ref, hid), (query_ref, que), (outg_ref, outg)))
    ]
    own_tests = pltpu.make_async_copy(
        test_ref, tests.at[pl.ds(pl.multiple_of(b * block_rows, block_rows), block_rows), :], t_sem
    )
    own_tests.start()
    for load in loads:
        load.start()

    barrier = pltpu.get_barrier_semaphore()
    partners = [to_sib, to_across, {"fsdp": beyond}, to_other]
    partners += [to_block(k) for k in range(1, blocks)]
    for to in partners:
        pl.semaphore_signal(barrier, inc=1, device_id=to, device_id_type=MESH)
    pl.semaphore_wait(barrier, len(partners))
    for h in range(AHEAD):
        send_own(h)
    for k in range(1, blocks):
        test_copy(k).start()

    loads[0].wait()
    strip = 16

    def normalize(i, carry):
        where = pl.ds(pl.multiple_of(i * strip, strip), strip)
        widened = hid[where, :].astype(jnp.float32)
        scale = lax.rsqrt(jnp.mean(widened * widened, axis=1, keepdims=True) + norm_eps)
        normed[where, :] = (widened * scale * gain_ref[...]).astype(jnp.bfloat16)
        return carry

    lax.fori_loop(0, hid.shape[0] // strip, normalize, 0)
    right[...] = lax.dot_general(
        normed[...], pin_ref[...], CONTRACT_LAST, preferred_element_type=jnp.float32
    )
    left[...] = jnp.zeros_like(left)
    loads[1].wait()
    loads[2].wait()

    def stack(ref, e, h):
        block = ref[e * SEQ : (e + 1) * SEQ, pl.ds(pl.multiple_of(h * GROUP * HEAD, HEAD), GROUP * HEAD)]
        return jnp.concatenate([block[:, i * HEAD : (i + 1) * HEAD] for i in range(GROUP)], axis=0)

    def head(h):
        weights = jnp.concatenate([wbuf[h, 0], wbuf[h, 1]], axis=1)
        both = jnp.dot(normed[...], weights, preferred_element_type=jnp.float32)
        cosine, sine = cos_ref[...], sin_ref[...]
        keys = both[:, :HEAD]
        keys = (keys * cosine + pltpu.roll(keys, HEAD // 2, 1) * sine).astype(jnp.bfloat16)
        values = both[:, HEAD:].astype(jnp.bfloat16)
        places = lax.broadcasted_iota(jnp.int32, (SEQ, GROUP * SEQ), 1) % SEQ
        causal = lax.broadcasted_iota(jnp.int32, (SEQ, GROUP * SEQ), 0) <= places
        grads = []
        for e in range(count):
            mine = slice(e * SEQ, (e + 1) * SEQ)
            queries = stack(que, e, h)
            logits = lax.dot_general(
                keys[mine], queries, CONTRACT_LAST, preferred_element_type=jnp.float32
            ) * inverse
            logits = jnp.where(causal, logits, -1e30)
            raised = jnp.exp(logits - jnp.max(logits, axis=0, keepdims=True))
            prob = raised / jnp.sum(raised, axis=0, keepdims=True)
            grad_prob = lax.dot_general(
                values[mine], stack(outg, e, h), CONTRACT_LAST, preferred_element_type=jnp.float32
            )
            grad_prob = jnp.where(places < len_ref[e], grad_prob, 0.0)
            total = jnp.sum(prob * grad_prob, axis=0, keepdims=True)
            grad_logit = (prob * (grad_prob - total)).astype(jnp.bfloat16)
            grads.append(jnp.dot(grad_logit, queries, preferred_element_type=jnp.float32))
        grad = jnp.concatenate(grads, axis=0) * inverse
        grad = grad * cosine + pltpu.roll(grad * sine, HEAD // 2, 1)
        block = pout_ref[:, pl.ds(pl.multiple_of(h * HEAD, HEAD), HEAD)]
        left[...] += lax.dot_general(
            grad.astype(jnp.bfloat16), block, CONTRACT_LAST, preferred_element_type=jnp.float32
        )

    def step(i, carry):
        @pl.when(i < KV_HEADS)
        def _():
            copy(i, rows_of(across, half), x_send, x_recv, to_across).wait_recv()
            copy(i, rows_of(across, half), y_send, y_recv, to_other).start()
            copy(i, rows_of(across, half), fx_send, fx_recv, to_sib).start()

        @pl.when(i + AHEAD < KV_HEADS)
        def _():
            send_own(i + AHEAD)

        @pl.when((i >= 1) & (i <= KV_HEADS))
        def _():
            copy(i - 1, rows_of(across, 1 - half), y_send, y_recv, to_other).wait_recv()
            copy(i - 1, rows_of(across, 1 - half), fy_send, fy_recv, to_sib).start()

        @pl.when(i >= 2)
        def _():
            h = i - 2
            copy(h, whole_sib, sib_send, sib_recv, to_sib).wait_recv()
            copy(h, rows_of(beyond, half), fx_send, fx_recv, to_sib).wait_recv()
            copy(h, rows_of(beyond, 1 - half), fy_send, fy_recv, to_sib).wait_recv()
            head(h)

        return carry

    lax.fori_loop(0, KV_HEADS + 2, step, 0)

    def finish(h, carry):
        copy(h, rows_of(f, half), x_send, x_recv, to_across).wait_send()
        copy(h, whole_own, sib_send, sib_recv, to_sib).wait_send()
        copy(h, rows_of(across, half), y_send, y_recv, to_other).wait_send()
        copy(h, rows_of(across, half), fx_send, fx_recv, to_sib).wait_send()
        copy(h, rows_of(across, 1 - half), fy_send, fy_recv, to_sib).wait_send()
        return carry

    lax.fori_loop(0, KV_HEADS, finish, 0)
    shape = (hid.shape[0], PROJ * count)
    repeats = lax.broadcasted_iota(jnp.int32, (PROJ, PROJ * count), 0) == (
        lax.broadcasted_iota(jnp.int32, (PROJ, PROJ * count), 1) // count
    )
    spread = jnp.dot(
        left[...], repeats.astype(jnp.float32), precision=HIGHEST, preferred_element_type=jnp.float32
    )
    belongs = lax.broadcasted_iota(jnp.int32, shape, 0) // SEQ == (
        lax.broadcasted_iota(jnp.int32, shape, 1) % count
    )
    outer = lax.dot_general(
        jnp.where(belongs, spread, 0.0),
        right[...],
        (((0,), (0,)), ((), ())),
        precision=HIGHEST,
        preferred_element_type=jnp.float32,
    )
    slot = f * blocks + b
    for i in range(PROJ):
        fbuf[slot, :, i * PROJ : (i + 1) * PROJ] = outer[i * count : (i + 1) * count, :]
    for k in range(1, blocks):
        feat_copy(k).start()
    for k in range(1, blocks):
        feat_copy(k).wait_recv()
    for k in range(1, 4):
        spread_copy(k).start()
    own_tests.wait()
    for k in range(1, blocks):
        test_copy(k).wait_recv()
    for k in range(1, 4):
        spread_copy(k).wait_recv()
    for i in range(4 * blocks):
        flat[i * count : (i + 1) * count, :] = fbuf[i]
    out_ref[...] = score(flat[...], tests[...], inv_ref, slot * count, count)
    for k in range(1, blocks):
        test_copy(k).wait_send()
        feat_copy(k).wait_send()
    for k in range(1, 4):
        spread_copy(k).wait_send()


def on_device(
    hidden, query, out_grad, lengths, gain, w_key, w_value, proj_in, proj_out, test_feats
):
    count = lengths.shape[0]
    tokens, width = hidden.shape
    blocks = lax.axis_size("blk")
    examples = 4 * blocks * count
    cosine, sine = rope_tables(count)
    anywhere = pl.BlockSpec(memory_space=pl.ANY)
    vmem = pl.BlockSpec(memory_space=pltpu.VMEM)
    smem = pl.BlockSpec(memory_space=pltpu.SMEM)
    heads = pltpu.SemaphoreType.DMA((KV_HEADS,))
    queries = blocks * test_feats.shape[0]
    return pl.pallas_call(
        score_kernel,
        out_shape=jax.ShapeDtypeStruct((count, queries), jnp.float32),
        in_specs=[anywhere] * 3 + [smem, vmem] + [anywhere] * 2 + [vmem] * 2 + [anywhere] + [vmem] * 2,
        out_specs=vmem,
        scratch_shapes=[
            pltpu.VMEM((KV_HEADS, 2, width, HEAD), jnp.bfloat16),
            pltpu.VMEM((tokens, width), jnp.bfloat16),
            pltpu.VMEM((tokens, query.shape[1]), jnp.bfloat16),
            pltpu.VMEM((tokens, query.shape[1]), jnp.bfloat16),
            pltpu.VMEM((tokens, width), jnp.bfloat16),
            pltpu.VMEM((tokens, PROJ), jnp.float32),
            pltpu.VMEM((tokens, PROJ), jnp.float32),
            pltpu.VMEM((4 * blocks, count, PROJ * PROJ), jnp.float32),
            pltpu.VMEM((examples, PROJ * PROJ), jnp.float32),
            pltpu.VMEM((queries, PROJ * PROJ), jnp.bfloat16),
            pltpu.VMEM((examples, examples), jnp.float32),
            pltpu.SemaphoreType.DMA((3,)),
            pltpu.SemaphoreType.DMA((2, KV_HEADS)),
        ]
        + [heads] * 10
        + [pltpu.SemaphoreType.DMA]
        + [pltpu.SemaphoreType.DMA((blocks,))] * 4
        + [pltpu.SemaphoreType.DMA((4,))] * 2,
        compiler_params=pltpu.CompilerParams(
            collective_id=0, has_side_effects=True, vmem_limit_bytes=58 * 1024 * 1024
        ),
        cost_estimate=pl.CostEstimate(
            flops=2 * tokens * width * 2 * KV_HEADS * HEAD, bytes_accessed=100_000_000, transcendentals=0
        ),
    )(
        hidden, query, out_grad, lengths, gain.reshape(1, width), w_key, w_value,
        proj_in.T, proj_out.T, test_feats, cosine, sine,
    )


def solution(mesh):
    in_specs = (
        P(("groups", "blk", "fsdp"), None),
        P(("groups", "blk", "fsdp"), None),
        P(("groups", "blk", "fsdp"), None),
        P(("groups", "blk", "fsdp")),
        P(),
        P("fsdp", None),
        P("fsdp", None),
        P(),
        P(),
        P("blk", None),
    )
    out_specs = P(("groups", "blk", "fsdp"), None)
    return jax.shard_map(
        on_device, mesh=mesh, in_specs=in_specs, out_specs=out_specs, check_vma=False
    )
```

```python
import math

import jax
import jax.numpy as jnp
import numpy as np
from jax import lax
from jax.experimental import pallas as pl
from jax.experimental.pallas import tpu as pltpu
from jax.sharding import PartitionSpec as P

HEADS = 32
KV_HEADS = 8
HEAD = 128
PROJ = 32
SEQ = 64


norm_eps = 1e-05
rope_base = 500000.0
damping = 0.01
GROUP = HEADS // KV_HEADS
AHEAD = 3
SIB, X, X_FAR, Y, Z, Y_FAR, S_X, S_X_FAR, S_Y, S_Z, S_Y_FAR = range(11)


def rope_tables(count):
    freqs = rope_base ** (-2.0 * np.arange(HEAD // 2) / HEAD)
    angles = np.arange(SEQ)[:, None] * freqs[None, :]
    cosine, sine = np.cos(angles), np.sin(angles)
    cosine = np.concatenate([cosine, cosine], -1)
    sine = np.concatenate([-sine, sine], -1)
    return [np.tile(table, (count, 1)).astype(np.float32) for table in (cosine, sine)]


HIGHEST = lax.Precision.HIGHEST
CONTRACT_LAST = (((1,), (1,)), ((), ()))


def sweep(system, row, col, k, lanes, subs):
    pivot = 1.0 / jnp.sum(jnp.where(lanes[:1] == k, row, 0.0), axis=1, keepdims=True)
    row = jnp.where(lanes[:1] == k, pivot, row * pivot)
    col = jnp.where(subs[:, :1] == k, -1.0, col)
    return jnp.where((lanes == k) | (subs == k), 0.0, system) - col * row


def score(feats, tests, inv_ref, first, mine):
    count, width = feats.shape
    gram = lax.dot_general(
        feats, feats, CONTRACT_LAST, precision=HIGHEST, preferred_element_type=jnp.float32
    )
    lanes = lax.broadcasted_iota(jnp.int32, (count, count), 1)
    subs = lax.broadcasted_iota(jnp.int32, (count, count), 0)
    diagonal = lanes == subs
    mean_diag = jnp.sum(jnp.where(diagonal, gram, 0.0), keepdims=True) / width + 1e-06
    system = gram / mean_diag + jnp.where(diagonal, damping, 0.0)
    if count <= 128:
        for k in range(count):
            system = sweep(system, system[k : k + 1, :], system[:, k : k + 1], k, lanes, subs)
        inv_ref[...] = system
    else:
        inv_ref[...] = system

        def step(k, carry):
            now = inv_ref[...]
            col = jnp.sum(jnp.where(lanes == k, now, 0.0), axis=1, keepdims=True)
            inv_ref[...] = sweep(now, inv_ref[pl.ds(k, 1), :], col, k, lanes, subs)
            return carry

        lax.fori_loop(0, count, step, 0)
    chosen = lax.broadcasted_iota(jnp.int32, (mine, count), 1) == (
        lax.broadcasted_iota(jnp.int32, (mine, count), 0) + first
    )
    rows = lax.dot_general(
        chosen.astype(jnp.float32),
        inv_ref[...],
        (((1,), (0,)), ((), ())),
        precision=HIGHEST,
        preferred_element_type=jnp.float32,
    )
    weighted = jnp.dot(rows, feats, precision=HIGHEST, preferred_element_type=jnp.float32)
    total = None
    for _ in range(3):
        piece = weighted.astype(jnp.bfloat16)
        weighted = weighted - piece.astype(jnp.float32)
        term = lax.dot_general(
            piece, tests, CONTRACT_LAST, preferred_element_type=jnp.float32
        )
        total = term if total is None else total + term
    return total


def score_kernel(
    hidden_ref, query_ref, outg_ref, len_ref, gain_ref, wk_ref, wv_ref, pin_ref, pout_ref,
    test_ref, cos_ref, sin_ref, out_ref,
    wbuf, hid, que, outg, normed, left, right, fbuf, flat, tests, inv_ref,
    in_sem, own_sem, sends, recvs, t_sem, t_send, t_recv, u_send, u_recv, a_send, a_recv, b_send, b_recv,
):
    count = len_ref.shape[0]
    rows = wk_ref.shape[0]
    eighth = rows // 8
    inverse = 1.0 / math.sqrt(HEAD)
    g = lax.axis_index("groups")
    f = lax.axis_index("fsdp")
    sib = f + 1 - 2 * (f % 2)
    across = (f + 2) % 4
    beyond = (sib + 2) % 4
    other = g + 1 - 2 * (g % 2)
    b = lax.axis_index("blk")
    blocks = lax.axis_size("blk")
    block_rows = test_ref.shape[0]
    MESH = pl.DeviceIdType.MESH

    def to_block(k):
        return {"blk": (b + k) % blocks}

    beside = b + 1 - 2 * (b % 2)
    half_block = block_rows // 2

    def test_rows(block):
        start = block * block_rows + (f % 2) * half_block
        return tests.at[pl.ds(pl.multiple_of(start, half_block), half_block), :]

    def test_copy(k):
        start = pl.multiple_of((f % 2) * half_block, half_block)
        return pltpu.make_async_remote_copy(
            src_ref=test_ref.at[pl.ds(start, half_block), :], dst_ref=test_rows(b),
            send_sem=t_send.at[k], recv_sem=t_recv.at[k], device_id=to_block(k), device_id_type=MESH,
        )

    def test_pass(k):
        part = test_rows((b + blocks - k) % blocks)
        return pltpu.make_async_remote_copy(
            src_ref=part, dst_ref=part, send_sem=u_send.at[k], recv_sem=u_recv.at[k],
            device_id=to_sib, device_id_type=MESH,
        )

    def feat_copy(k):
        part = fbuf.at[f * blocks + b]
        return pltpu.make_async_remote_copy(
            src_ref=part, dst_ref=part, send_sem=a_send.at[k],
            recv_sem=a_recv.at[k], device_id=to_block(k), device_id_type=MESH,
        )

    def spread_copy(k):
        part = fbuf.at[pl.ds(f * blocks, blocks)]
        return pltpu.make_async_remote_copy(
            src_ref=part, dst_ref=part, send_sem=b_send.at[k],
            recv_sem=b_recv.at[k], device_id={"fsdp": (f + k) % 4}, device_id_type=MESH,
        )

    mine = 2 * (g % 2) + b % 2
    by_y = 2 * (1 - g % 2) + b % 2
    by_z = 2 * (g % 2) + 1 - b % 2
    far = 2 * (1 - g % 2) + 1 - b % 2

    def rows_of(owner, quarter, part=None):
        start = owner * rows + quarter * 2 * eighth + (part or 0) * eighth
        return pl.ds(pl.multiple_of(start, eighth), eighth * (2 if part is None else 1))

    def copy(h, where, kind, to):
        part = wbuf.at[h, :, where, :]
        return pltpu.make_async_remote_copy(
            src_ref=part, dst_ref=part, send_sem=sends.at[kind, h], recv_sem=recvs.at[kind, h],
            device_id=to, device_id_type=MESH,
        )

    whole_own = pl.ds(pl.multiple_of(f * rows, rows), rows)
    whole_sib = pl.ds(pl.multiple_of(sib * rows, rows), rows)
    to_sib, to_across = {"fsdp": sib}, {"fsdp": across}
    to_other, to_beside = {"groups": other}, {"blk": beside}
    sent = {
        SIB: (whole_own, to_sib),
        X: (rows_of(f, mine), to_across),
        X_FAR: (rows_of(f, far, 0), to_across),
        Y: (rows_of(across, mine), to_other),
        Z: (rows_of(across, mine), to_beside),
        Y_FAR: (rows_of(across, by_z, 1), to_other),
        S_X: (rows_of(across, mine), to_sib),
        S_X_FAR: (rows_of(across, far, 0), to_sib),
        S_Y: (rows_of(across, by_y), to_sib),
        S_Z: (rows_of(across, by_z), to_sib),
        S_Y_FAR: (rows_of(across, far, 1), to_sib),
    }
    received = {
        SIB: whole_sib,
        X: rows_of(across, mine),
        X_FAR: rows_of(across, far, 0),
        Y: rows_of(across, by_y),
        Z: rows_of(across, by_z),
        Y_FAR: rows_of(across, far, 1),
        S_X: rows_of(beyond, mine),
        S_X_FAR: rows_of(beyond, far, 0),
        S_Y: rows_of(beyond, by_y),
        S_Z: rows_of(beyond, by_z),
        S_Y_FAR: rows_of(beyond, far, 1),
    }

    def start(h, *kinds):
        for kind in kinds:
            where, to = sent[kind]
            copy(h, where, kind, to).start()

    def arrive(h, *kinds):
        for kind in kinds:
            copy(h, received[kind], kind, sent[kind][1]).wait_recv()

    def own(h, kind):
        return pltpu.make_async_copy(
            (wk_ref, wv_ref)[kind].at[:, pl.ds(pl.multiple_of(h * HEAD, HEAD), HEAD)],
            wbuf.at[h, kind, whole_own, :],
            own_sem.at[kind, h],
        )

    def send_own(h):
        own(h, 0).wait()
        own(h, 1).wait()
        start(h, X, X_FAR, SIB)

    def start_own(h, carry):
        own(h, 0).start()
        own(h, 1).start()
        return carry

    barrier = pltpu.get_barrier_semaphore()
    partners = [to_sib, to_across, {"fsdp": beyond}, to_other]
    partners += [to_block(k) for k in range(1, blocks)]
    for to in partners:
        pl.semaphore_signal(barrier, inc=1, device_id=to, device_id_type=MESH)
    lax.fori_loop(0, KV_HEADS, start_own, 0)
    loads = [
        pltpu.make_async_copy(src, dst, in_sem.at[i])
        for i, (src, dst) in enumerate(((hidden_ref, hid), (query_ref, que), (outg_ref, outg)))
    ]
    own_tests = pltpu.make_async_copy(
        test_ref, tests.at[pl.ds(pl.multiple_of(b * block_rows, block_rows), block_rows), :], t_sem
    )
    own_tests.start()
    for load in loads:
        load.start()

    pl.semaphore_wait(barrier, len(partners))
    for h in range(AHEAD):
        send_own(h)

    loads[0].wait()
    strip = 16

    def normalize(i, carry):
        where = pl.ds(pl.multiple_of(i * strip, strip), strip)
        widened = hid[where, :].astype(jnp.float32)
        scale = lax.rsqrt(jnp.mean(widened * widened, axis=1, keepdims=True) + norm_eps)
        normed[where, :] = (widened * scale * gain_ref[...]).astype(jnp.bfloat16)
        return carry

    lax.fori_loop(0, hid.shape[0] // strip, normalize, 0)
    right[...] = lax.dot_general(
        normed[...], pin_ref[...], CONTRACT_LAST, preferred_element_type=jnp.float32
    )
    left[...] = jnp.zeros_like(left)
    loads[1].wait()
    loads[2].wait()

    def stack(ref, e, h):
        block = ref[e * SEQ : (e + 1) * SEQ, pl.ds(pl.multiple_of(h * GROUP * HEAD, HEAD), GROUP * HEAD)]
        return jnp.concatenate([block[:, i * HEAD : (i + 1) * HEAD] for i in range(GROUP)], axis=0)

    def head(h):
        weights = jnp.concatenate([wbuf[h, 0], wbuf[h, 1]], axis=1)
        both = jnp.dot(normed[...], weights, preferred_element_type=jnp.float32)
        cosine, sine = cos_ref[...], sin_ref[...]
        keys = both[:, :HEAD]
        keys = (keys * cosine + pltpu.roll(keys, HEAD // 2, 1) * sine).astype(jnp.bfloat16)
        values = both[:, HEAD:].astype(jnp.bfloat16)
        places = lax.broadcasted_iota(jnp.int32, (SEQ, GROUP * SEQ), 1) % SEQ
        causal = lax.broadcasted_iota(jnp.int32, (SEQ, GROUP * SEQ), 0) <= places
        grads = []
        for e in range(count):
            mine = slice(e * SEQ, (e + 1) * SEQ)
            queries = stack(que, e, h)
            logits = lax.dot_general(
                keys[mine], queries, CONTRACT_LAST, preferred_element_type=jnp.float32
            ) * inverse
            logits = jnp.where(causal, logits, -1e30)
            raised = jnp.exp(logits - jnp.max(logits, axis=0, keepdims=True))
            prob = raised / jnp.sum(raised, axis=0, keepdims=True)
            grad_prob = lax.dot_general(
                values[mine], stack(outg, e, h), CONTRACT_LAST, preferred_element_type=jnp.float32
            )
            grad_prob = jnp.where(places < len_ref[e], grad_prob, 0.0)
            total = jnp.sum(prob * grad_prob, axis=0, keepdims=True)
            grad_logit = (prob * (grad_prob - total)).astype(jnp.bfloat16)
            grads.append(jnp.dot(grad_logit, queries, preferred_element_type=jnp.float32))
        grad = jnp.concatenate(grads, axis=0) * inverse
        grad = grad * cosine + pltpu.roll(grad * sine, HEAD // 2, 1)
        block = pout_ref[:, pl.ds(pl.multiple_of(h * HEAD, HEAD), HEAD)]
        left[...] += lax.dot_general(
            grad.astype(jnp.bfloat16), block, CONTRACT_LAST, preferred_element_type=jnp.float32
        )

    def step(i, carry):
        @pl.when(i < KV_HEADS)
        def _():
            arrive(i, X)
            start(i, Y, Z, S_X)
            arrive(i, X_FAR)
            start(i, S_X_FAR)

        @pl.when(i + AHEAD < KV_HEADS)
        def _():
            send_own(i + AHEAD)

        @pl.when(i == KV_HEADS // 2)
        def _():
            for k in range(1, blocks):
                test_copy(k).start()

        @pl.when((i >= 1) & (i <= KV_HEADS))
        def _():
            arrive(i - 1, Z)
            start(i - 1, Y_FAR, S_Z)
            arrive(i - 1, Y)
            start(i - 1, S_Y)

        @pl.when(i > KV_HEADS)
        def _():
            for k in range(1, blocks):
                test_copy(k).wait_recv()
                test_pass(k).start()

        @pl.when(i >= 2)
        def _():
            h = i - 2
            arrive(h, Y_FAR)
            start(h, S_Y_FAR)
            arrive(h, SIB, S_X, S_X_FAR, S_Y, S_Z, S_Y_FAR)
            head(h)

        return carry

    lax.fori_loop(0, KV_HEADS + 2, step, 0)

    def finish(h, carry):
        for kind, (where, to) in sent.items():
            copy(h, where, kind, to).wait_send()
        return carry

    lax.fori_loop(0, KV_HEADS, finish, 0)
    shape = (hid.shape[0], PROJ * count)
    repeats = lax.broadcasted_iota(jnp.int32, (PROJ, PROJ * count), 0) == (
        lax.broadcasted_iota(jnp.int32, (PROJ, PROJ * count), 1) // count
    )
    spread = jnp.dot(
        left[...], repeats.astype(jnp.float32), precision=HIGHEST, preferred_element_type=jnp.float32
    )
    belongs = lax.broadcasted_iota(jnp.int32, shape, 0) // SEQ == (
        lax.broadcasted_iota(jnp.int32, shape, 1) % count
    )
    outer = lax.dot_general(
        jnp.where(belongs, spread, 0.0),
        right[...],
        (((0,), (0,)), ((), ())),
        precision=HIGHEST,
        preferred_element_type=jnp.float32,
    )
    slot = f * blocks + b
    for i in range(PROJ):
        fbuf[slot, :, i * PROJ : (i + 1) * PROJ] = outer[i * count : (i + 1) * count, :]
    for k in range(1, blocks):
        feat_copy(k).start()
    for k in range(1, blocks):
        feat_copy(k).wait_recv()
    for k in range(1, 4):
        spread_copy(k).start()
    own_tests.wait()
    for k in range(1, blocks):
        test_pass(k).wait_recv()
    for k in range(1, 4):
        spread_copy(k).wait_recv()
    for i in range(4 * blocks):
        flat[i * count : (i + 1) * count, :] = fbuf[i]
    out_ref[...] = score(flat[...], tests[...], inv_ref, slot * count, count)
    for k in range(1, blocks):
        test_copy(k).wait_send()
        test_pass(k).wait_send()
        feat_copy(k).wait_send()
    for k in range(1, 4):
        spread_copy(k).wait_send()


def on_device(
    hidden, query, out_grad, lengths, gain, w_key, w_value, proj_in, proj_out, test_feats
):
    count = lengths.shape[0]
    tokens, width = hidden.shape
    blocks = lax.axis_size("blk")
    examples = 4 * blocks * count
    cosine, sine = rope_tables(count)
    anywhere = pl.BlockSpec(memory_space=pl.ANY)
    vmem = pl.BlockSpec(memory_space=pltpu.VMEM)
    smem = pl.BlockSpec(memory_space=pltpu.SMEM)
    queries = blocks * test_feats.shape[0]
    return pl.pallas_call(
        score_kernel,
        out_shape=jax.ShapeDtypeStruct((count, queries), jnp.float32),
        in_specs=[anywhere] * 3 + [smem, vmem] + [anywhere] * 2 + [vmem] * 2 + [anywhere] + [vmem] * 2,
        out_specs=vmem,
        scratch_shapes=[
            pltpu.VMEM((KV_HEADS, 2, width, HEAD), jnp.bfloat16),
            pltpu.VMEM((tokens, width), jnp.bfloat16),
            pltpu.VMEM((tokens, query.shape[1]), jnp.bfloat16),
            pltpu.VMEM((tokens, query.shape[1]), jnp.bfloat16),
            pltpu.VMEM((tokens, width), jnp.bfloat16),
            pltpu.VMEM((tokens, PROJ), jnp.float32),
            pltpu.VMEM((tokens, PROJ), jnp.float32),
            pltpu.VMEM((4 * blocks, count, PROJ * PROJ), jnp.float32),
            pltpu.VMEM((examples, PROJ * PROJ), jnp.float32),
            pltpu.VMEM((queries, PROJ * PROJ), jnp.bfloat16),
            pltpu.VMEM((examples, examples), jnp.float32),
            pltpu.SemaphoreType.DMA((3,)),
            pltpu.SemaphoreType.DMA((2, KV_HEADS)),
        ]
        + [pltpu.SemaphoreType.DMA((11, KV_HEADS))] * 2
        + [pltpu.SemaphoreType.DMA]
        + [pltpu.SemaphoreType.DMA((blocks,))] * 6
        + [pltpu.SemaphoreType.DMA((4,))] * 2,
        compiler_params=pltpu.CompilerParams(
            collective_id=0, has_side_effects=True, vmem_limit_bytes=58 * 1024 * 1024
        ),
        cost_estimate=pl.CostEstimate(
            flops=2 * tokens * width * 2 * KV_HEADS * HEAD, bytes_accessed=100_000_000, transcendentals=0
        ),
    )(
        hidden, query, out_grad, lengths, gain.reshape(1, width), w_key, w_value,
        proj_in.T, proj_out.T, test_feats, cosine, sine,
    )


def solution(mesh):
    in_specs = (
        P(("groups", "blk", "fsdp"), None),
        P(("groups", "blk", "fsdp"), None),
        P(("groups", "blk", "fsdp"), None),
        P(("groups", "blk", "fsdp")),
        P(),
        P("fsdp", None),
        P("fsdp", None),
        P(),
        P(),
        P("blk", None),
    )
    out_specs = P(("groups", "blk", "fsdp"), None)
    return jax.shard_map(
        on_device, mesh=mesh, in_specs=in_specs, out_specs=out_specs, check_vma=False
    )
```

```python
import math

import jax
import jax.numpy as jnp
import numpy as np
from jax import lax
from jax.experimental import pallas as pl
from jax.experimental.pallas import tpu as pltpu
from jax.sharding import PartitionSpec as P

HEADS = 32
KV_HEADS = 8
HEAD = 128
PROJ = 32
SEQ = 64


norm_eps = 1e-05
rope_base = 500000.0
damping = 0.01
GROUP = HEADS // KV_HEADS
AHEAD = 3
SIB, X, X_FAR, Y, Z, Y_FAR, S_X, S_X_FAR, S_Y, S_Z, S_Y_FAR = range(11)


def rope_tables(count):
    freqs = rope_base ** (-2.0 * np.arange(HEAD // 2) / HEAD)
    angles = np.arange(SEQ)[:, None] * freqs[None, :]
    cosine, sine = np.cos(angles), np.sin(angles)
    cosine = np.concatenate([cosine, cosine], -1)
    sine = np.concatenate([-sine, sine], -1)
    return [np.tile(table, (count, 1)).astype(np.float32) for table in (cosine, sine)]


HIGHEST = lax.Precision.HIGHEST
CONTRACT_LAST = (((1,), (1,)), ((), ()))


def sweep(system, row, col, k, lanes, subs):
    pivot = 1.0 / jnp.sum(jnp.where(lanes[:1] == k, row, 0.0), axis=1, keepdims=True)
    row = jnp.where(lanes[:1] == k, pivot, row * pivot)
    col = jnp.where(subs[:, :1] == k, -1.0, col)
    return jnp.where((lanes == k) | (subs == k), 0.0, system) - col * row


def score(feats, tests, inv_ref, first, mine):
    count, width = feats.shape
    gram = lax.dot_general(
        feats, feats, CONTRACT_LAST, precision=HIGHEST, preferred_element_type=jnp.float32
    )
    lanes = lax.broadcasted_iota(jnp.int32, (count, count), 1)
    subs = lax.broadcasted_iota(jnp.int32, (count, count), 0)
    diagonal = lanes == subs
    mean_diag = jnp.sum(jnp.where(diagonal, gram, 0.0), keepdims=True) / width + 1e-06
    system = gram / mean_diag + jnp.where(diagonal, damping, 0.0)
    if count <= 128:
        for k in range(count):
            system = sweep(system, system[k : k + 1, :], system[:, k : k + 1], k, lanes, subs)
        inv_ref[...] = system
    else:
        inv_ref[...] = system

        def step(k, carry):
            now = inv_ref[...]
            col = jnp.sum(jnp.where(lanes == k, now, 0.0), axis=1, keepdims=True)
            inv_ref[...] = sweep(now, inv_ref[pl.ds(k, 1), :], col, k, lanes, subs)
            return carry

        lax.fori_loop(0, count, step, 0)
    chosen = lax.broadcasted_iota(jnp.int32, (mine, count), 1) == (
        lax.broadcasted_iota(jnp.int32, (mine, count), 0) + first
    )
    rows = lax.dot_general(
        chosen.astype(jnp.float32),
        inv_ref[...],
        (((1,), (0,)), ((), ())),
        precision=HIGHEST,
        preferred_element_type=jnp.float32,
    )
    weighted = jnp.dot(rows, feats, precision=HIGHEST, preferred_element_type=jnp.float32)
    total = None
    for _ in range(3):
        piece = weighted.astype(jnp.bfloat16)
        weighted = weighted - piece.astype(jnp.float32)
        term = lax.dot_general(
            piece, tests, CONTRACT_LAST, preferred_element_type=jnp.float32
        )
        total = term if total is None else total + term
    return total


def score_kernel(
    hidden_ref, query_ref, outg_ref, len_ref, gain_ref, wk_ref, wv_ref, pin_ref, pout_ref,
    test_ref, cos_ref, sin_ref, out_ref,
    wbuf, hid, que, outg, normed, left, right, fbuf, flat, tests, inv_ref,
    in_sem, own_sem, sends, recvs, t_sem, t_send, t_recv, u_send, u_recv, a_send, a_recv, b_send, b_recv,
):
    count = len_ref.shape[0]
    rows = wk_ref.shape[0]
    eighth = rows // 8
    inverse = 1.0 / math.sqrt(HEAD)
    g = lax.axis_index("groups")
    f = lax.axis_index("fsdp")
    sib = f + 1 - 2 * (f % 2)
    across = (f + 2) % 4
    beyond = (sib + 2) % 4
    other = g + 1 - 2 * (g % 2)
    b = lax.axis_index("blk")
    blocks = lax.axis_size("blk")
    block_rows = test_ref.shape[0]
    MESH = pl.DeviceIdType.MESH

    def to_block(k):
        return {"blk": (b + k) % blocks}

    beside = b + 1 - 2 * (b % 2)
    half_block = block_rows // 2

    def test_rows(block):
        start = block * block_rows + (f % 2) * half_block
        return tests.at[pl.ds(pl.multiple_of(start, half_block), half_block), :]

    def test_copy(k):
        start = pl.multiple_of((f % 2) * half_block, half_block)
        return pltpu.make_async_remote_copy(
            src_ref=test_ref.at[pl.ds(start, half_block), :], dst_ref=test_rows(b),
            send_sem=t_send.at[k], recv_sem=t_recv.at[k], device_id=to_block(k), device_id_type=MESH,
        )

    def test_pass(k):
        part = test_rows((b + blocks - k) % blocks)
        return pltpu.make_async_remote_copy(
            src_ref=part, dst_ref=part, send_sem=u_send.at[k], recv_sem=u_recv.at[k],
            device_id=to_sib, device_id_type=MESH,
        )

    def feat_copy(k):
        part = fbuf.at[f * blocks + b]
        return pltpu.make_async_remote_copy(
            src_ref=part, dst_ref=part, send_sem=a_send.at[k],
            recv_sem=a_recv.at[k], device_id=to_block(k), device_id_type=MESH,
        )

    def spread_copy(k):
        part = fbuf.at[pl.ds(f * blocks, blocks)]
        return pltpu.make_async_remote_copy(
            src_ref=part, dst_ref=part, send_sem=b_send.at[k],
            recv_sem=b_recv.at[k], device_id={"fsdp": (f + k) % 4}, device_id_type=MESH,
        )

    mine = 2 * (g % 2) + b % 2
    by_y = 2 * (1 - g % 2) + b % 2
    by_z = 2 * (g % 2) + 1 - b % 2
    far = 2 * (1 - g % 2) + 1 - b % 2

    def rows_of(owner, quarter, part=None):
        start = owner * rows + quarter * 2 * eighth + (part or 0) * eighth
        return pl.ds(pl.multiple_of(start, eighth), eighth * (2 if part is None else 1))

    def copy(h, where, kind, to):
        part = wbuf.at[h, :, where, :]
        return pltpu.make_async_remote_copy(
            src_ref=part, dst_ref=part, send_sem=sends.at[kind, h], recv_sem=recvs.at[kind, h],
            device_id=to, device_id_type=MESH,
        )

    whole_own = pl.ds(pl.multiple_of(f * rows, rows), rows)
    whole_sib = pl.ds(pl.multiple_of(sib * rows, rows), rows)
    to_sib, to_across = {"fsdp": sib}, {"fsdp": across}
    to_other, to_beside = {"groups": other}, {"blk": beside}
    sent = {
        SIB: (whole_own, to_sib),
        X: (rows_of(f, mine), to_across),
        X_FAR: (rows_of(f, far, 0), to_across),
        Y: (rows_of(across, mine), to_other),
        Z: (rows_of(across, mine), to_beside),
        Y_FAR: (rows_of(across, by_z, 1), to_other),
        S_X: (rows_of(across, mine), to_sib),
        S_X_FAR: (rows_of(across, far, 0), to_sib),
        S_Y: (rows_of(across, by_y), to_sib),
        S_Z: (rows_of(across, by_z), to_sib),
        S_Y_FAR: (rows_of(across, far, 1), to_sib),
    }
    received = {
        SIB: whole_sib,
        X: rows_of(across, mine),
        X_FAR: rows_of(across, far, 0),
        Y: rows_of(across, by_y),
        Z: rows_of(across, by_z),
        Y_FAR: rows_of(across, far, 1),
        S_X: rows_of(beyond, mine),
        S_X_FAR: rows_of(beyond, far, 0),
        S_Y: rows_of(beyond, by_y),
        S_Z: rows_of(beyond, by_z),
        S_Y_FAR: rows_of(beyond, far, 1),
    }

    def start(h, *kinds):
        for kind in kinds:
            where, to = sent[kind]
            copy(h, where, kind, to).start()

    def arrive(h, *kinds):
        for kind in kinds:
            copy(h, received[kind], kind, sent[kind][1]).wait_recv()

    def own(h, kind):
        return pltpu.make_async_copy(
            (wk_ref, wv_ref)[kind].at[:, pl.ds(pl.multiple_of(h * HEAD, HEAD), HEAD)],
            wbuf.at[h, kind, whole_own, :],
            own_sem.at[kind, h],
        )

    def send_own(h):
        own(h, 0).wait()
        own(h, 1).wait()
        start(h, X, X_FAR, SIB)

    def start_own(h, carry):
        own(h, 0).start()
        own(h, 1).start()
        return carry

    barrier = pltpu.get_barrier_semaphore()
    partners = [to_sib, to_across, {"fsdp": beyond}, to_other]
    partners += [to_block(k) for k in range(1, blocks)]
    for to in partners:
        pl.semaphore_signal(barrier, inc=1, device_id=to, device_id_type=MESH)
    lax.fori_loop(0, KV_HEADS, start_own, 0)
    loads = [
        pltpu.make_async_copy(src, dst, in_sem.at[i])
        for i, (src, dst) in enumerate(((hidden_ref, hid), (query_ref, que), (outg_ref, outg)))
    ]
    own_tests = pltpu.make_async_copy(
        test_ref, tests.at[pl.ds(pl.multiple_of(b * block_rows, block_rows), block_rows), :], t_sem
    )
    own_tests.start()
    for load in loads:
        load.start()

    pl.semaphore_wait(barrier, len(partners))
    for h in range(AHEAD):
        send_own(h)

    loads[0].wait()
    strip = 16

    def normalize(i, carry):
        where = pl.ds(pl.multiple_of(i * strip, strip), strip)
        widened = hid[where, :].astype(jnp.float32)
        scale = lax.rsqrt(jnp.mean(widened * widened, axis=1, keepdims=True) + norm_eps)
        normed[where, :] = (widened * scale * gain_ref[...]).astype(jnp.bfloat16)
        return carry

    lax.fori_loop(0, hid.shape[0] // strip, normalize, 0)
    right[...] = lax.dot_general(
        normed[...], pin_ref[...], CONTRACT_LAST, preferred_element_type=jnp.float32
    )
    left[...] = jnp.zeros_like(left)
    loads[1].wait()
    loads[2].wait()

    def stack(ref, e, h):
        block = ref[e * SEQ : (e + 1) * SEQ, pl.ds(pl.multiple_of(h * GROUP * HEAD, HEAD), GROUP * HEAD)]
        return jnp.concatenate([block[:, i * HEAD : (i + 1) * HEAD] for i in range(GROUP)], axis=0)

    def head(h):
        weights = jnp.concatenate([wbuf[h, 0], wbuf[h, 1]], axis=1)
        both = jnp.dot(normed[...], weights, preferred_element_type=jnp.float32)
        cosine, sine = cos_ref[...], sin_ref[...]
        keys = both[:, :HEAD]
        keys = (keys * cosine + pltpu.roll(keys, HEAD // 2, 1) * sine).astype(jnp.bfloat16)
        values = both[:, HEAD:].astype(jnp.bfloat16)
        places = lax.broadcasted_iota(jnp.int32, (SEQ, GROUP * SEQ), 1) % SEQ
        causal = lax.broadcasted_iota(jnp.int32, (SEQ, GROUP * SEQ), 0) <= places
        grads = []
        for e in range(count):
            mine = slice(e * SEQ, (e + 1) * SEQ)
            queries = stack(que, e, h)
            logits = lax.dot_general(
                keys[mine], queries, CONTRACT_LAST, preferred_element_type=jnp.float32
            ) * inverse
            logits = jnp.where(causal, logits, -1e30)
            raised = jnp.exp(logits - jnp.max(logits, axis=0, keepdims=True))
            prob = raised / jnp.sum(raised, axis=0, keepdims=True)
            grad_prob = lax.dot_general(
                values[mine], stack(outg, e, h), CONTRACT_LAST, preferred_element_type=jnp.float32
            )
            grad_prob = jnp.where(places < len_ref[e], grad_prob, 0.0)
            total = jnp.sum(prob * grad_prob, axis=0, keepdims=True)
            grad_logit = (prob * (grad_prob - total)).astype(jnp.bfloat16)
            grads.append(jnp.dot(grad_logit, queries, preferred_element_type=jnp.float32))
        grad = jnp.concatenate(grads, axis=0) * inverse
        grad = grad * cosine + pltpu.roll(grad * sine, HEAD // 2, 1)
        block = pout_ref[:, pl.ds(pl.multiple_of(h * HEAD, HEAD), HEAD)]
        left[...] += lax.dot_general(
            grad.astype(jnp.bfloat16), block, CONTRACT_LAST, preferred_element_type=jnp.float32
        )

    def step(i, carry):
        @pl.when(i < KV_HEADS)
        def _():
            arrive(i, X)
            start(i, Y, Z, S_X)
            arrive(i, X_FAR)
            start(i, S_X_FAR)

        @pl.when(i + AHEAD < KV_HEADS)
        def _():
            send_own(i + AHEAD)

        @pl.when(i == KV_HEADS // 2)
        def _():
            for k in range(1, blocks):
                test_copy(k).start()

        @pl.when((i >= 2) & (i < KV_HEADS + 2))
        def _():
            arrive(i - 2, Z)
            start(i - 2, Y_FAR, S_Z)
            arrive(i - 2, Y)
            start(i - 2, S_Y)

        @pl.when(i == KV_HEADS + 1)
        def _():
            for k in range(1, blocks):
                test_copy(k).wait_recv()
                test_pass(k).start()

        @pl.when((i >= 3) & (i < KV_HEADS + 3))
        def _():
            h = i - 3
            arrive(h, Y_FAR)
            start(h, S_Y_FAR)

        @pl.when(i >= 4)
        def _():
            h = i - 4
            arrive(h, SIB, S_X, S_X_FAR, S_Y, S_Z, S_Y_FAR)
            head(h)

        return carry

    lax.fori_loop(0, KV_HEADS + 4, step, 0)

    def finish(h, carry):
        for kind, (where, to) in sent.items():
            copy(h, where, kind, to).wait_send()
        return carry

    lax.fori_loop(0, KV_HEADS, finish, 0)
    shape = (hid.shape[0], PROJ * count)
    repeats = lax.broadcasted_iota(jnp.int32, (PROJ, PROJ * count), 0) == (
        lax.broadcasted_iota(jnp.int32, (PROJ, PROJ * count), 1) // count
    )
    spread = jnp.dot(
        left[...], repeats.astype(jnp.float32), precision=HIGHEST, preferred_element_type=jnp.float32
    )
    belongs = lax.broadcasted_iota(jnp.int32, shape, 0) // SEQ == (
        lax.broadcasted_iota(jnp.int32, shape, 1) % count
    )
    outer = lax.dot_general(
        jnp.where(belongs, spread, 0.0),
        right[...],
        (((0,), (0,)), ((), ())),
        precision=HIGHEST,
        preferred_element_type=jnp.float32,
    )
    slot = f * blocks + b
    for i in range(PROJ):
        fbuf[slot, :, i * PROJ : (i + 1) * PROJ] = outer[i * count : (i + 1) * count, :]
    for k in range(1, blocks):
        feat_copy(k).start()
    for k in range(1, blocks):
        feat_copy(k).wait_recv()
    for k in range(1, 4):
        spread_copy(k).start()
    own_tests.wait()
    for k in range(1, blocks):
        test_pass(k).wait_recv()
    for k in range(1, 4):
        spread_copy(k).wait_recv()
    for i in range(4 * blocks):
        flat[i * count : (i + 1) * count, :] = fbuf[i]
    out_ref[...] = score(flat[...], tests[...], inv_ref, slot * count, count)
    for k in range(1, blocks):
        test_copy(k).wait_send()
        test_pass(k).wait_send()
        feat_copy(k).wait_send()
    for k in range(1, 4):
        spread_copy(k).wait_send()


def on_device(
    hidden, query, out_grad, lengths, gain, w_key, w_value, proj_in, proj_out, test_feats
):
    count = lengths.shape[0]
    tokens, width = hidden.shape
    blocks = lax.axis_size("blk")
    examples = 4 * blocks * count
    cosine, sine = rope_tables(count)
    anywhere = pl.BlockSpec(memory_space=pl.ANY)
    vmem = pl.BlockSpec(memory_space=pltpu.VMEM)
    smem = pl.BlockSpec(memory_space=pltpu.SMEM)
    queries = blocks * test_feats.shape[0]
    return pl.pallas_call(
        score_kernel,
        out_shape=jax.ShapeDtypeStruct((count, queries), jnp.float32),
        in_specs=[anywhere] * 3 + [smem, vmem] + [anywhere] * 2 + [vmem] * 2 + [anywhere] + [vmem] * 2,
        out_specs=vmem,
        scratch_shapes=[
            pltpu.VMEM((KV_HEADS, 2, width, HEAD), jnp.bfloat16),
            pltpu.VMEM((tokens, width), jnp.bfloat16),
            pltpu.VMEM((tokens, query.shape[1]), jnp.bfloat16),
            pltpu.VMEM((tokens, query.shape[1]), jnp.bfloat16),
            pltpu.VMEM((tokens, width), jnp.bfloat16),
            pltpu.VMEM((tokens, PROJ), jnp.float32),
            pltpu.VMEM((tokens, PROJ), jnp.float32),
            pltpu.VMEM((4 * blocks, count, PROJ * PROJ), jnp.float32),
            pltpu.VMEM((examples, PROJ * PROJ), jnp.float32),
            pltpu.VMEM((queries, PROJ * PROJ), jnp.bfloat16),
            pltpu.VMEM((examples, examples), jnp.float32),
            pltpu.SemaphoreType.DMA((3,)),
            pltpu.SemaphoreType.DMA((2, KV_HEADS)),
        ]
        + [pltpu.SemaphoreType.DMA((11, KV_HEADS))] * 2
        + [pltpu.SemaphoreType.DMA]
        + [pltpu.SemaphoreType.DMA((blocks,))] * 6
        + [pltpu.SemaphoreType.DMA((4,))] * 2,
        compiler_params=pltpu.CompilerParams(
            collective_id=0, has_side_effects=True, vmem_limit_bytes=58 * 1024 * 1024
        ),
        cost_estimate=pl.CostEstimate(
            flops=2 * tokens * width * 2 * KV_HEADS * HEAD, bytes_accessed=100_000_000, transcendentals=0
        ),
    )(
        hidden, query, out_grad, lengths, gain.reshape(1, width), w_key, w_value,
        proj_in.T, proj_out.T, test_feats, cosine, sine,
    )


def solution(mesh):
    in_specs = (
        P(("groups", "blk", "fsdp"), None),
        P(("groups", "blk", "fsdp"), None),
        P(("groups", "blk", "fsdp"), None),
        P(("groups", "blk", "fsdp")),
        P(),
        P("fsdp", None),
        P("fsdp", None),
        P(),
        P(),
        P("blk", None),
    )
    out_specs = P(("groups", "blk", "fsdp"), None)
    return jax.shard_map(
        on_device, mesh=mesh, in_specs=in_specs, out_specs=out_specs, check_vma=False
    )
```
